32 devices in a mesh: grp: 2 (over x), row: 2 (over core), col: 8 (over z, y).
Axes of the slice: x: 2, y: 2, z: 4, core: 2. Of those that a mesh axis runs over, the one named last changes fastest.
Arguments:
- hidden_acts: bfloat16 [512, 26624], P(('grp', 'row'), 'col'), parts along dimension 0, may hold values from -216 to 216
- down_weight: bfloat16 [26624, 8192], P('col', 'row'), may hold values from -0.0390625 to 0.0390625
- amax_history: float32 [8], P('grp'), parts along dimension 0, may hold values from 3 to 12
Outputs:
- scaled_out: bfloat16 [512, 8192], P(('grp', 'col'), 'row'), parts along dimension 0
- token_scale: float32 [512], P(('grp', 'row')), parts along dimension 0
- history_next: float32 [8], P('grp'), parts along dimension 0
The draws below stay inside these ranges and needn't reach their ends.
There are 2 independent parts, one for each index of `grp`. The reference program is written for one: setup_inputs(seed, part) draws one part's arguments, and reference() takes and returns one part's arrays. A program takes and returns all parts, laid end to end along the dimension named above; an argument that names none is the same for every part. Nothing has to cross between parts.
All inputs are finite; a program needn't handle non-finite values.
Results may differ from the reference program's by a relative error of at most 0.0044.
Values may be sent and summed in bfloat16 or wider, within the bound.
A program may use at most 64 MiB of HBM per device.

```python
import math
import jax
import jax.numpy as jnp
from jax import lax

D = 8192
F = 26624
HIST = 4
TOKENS_BLK = 32
TOKENS = 256
F_BLK = 3328


def draw_hidden_acts(key, part):
    key_vals = jax.random.fold_in(key, 11)
    key_rows = jax.random.fold_in(key, 12)
    key_cols = jax.random.fold_in(key, 13)
    key_order = jax.random.fold_in(key, 14)
    key_place = jax.random.fold_in(key, 15)
    key_where = jax.random.fold_in(key, 16)
    key_signs = jax.random.fold_in(key, 17)
    key_heavy = jax.random.fold_in(key, 18)
    key_posit = jax.random.fold_in(key, 19)
    blocks = TOKENS // TOKENS_BLK
    quiet_count = max(1, blocks // 4)
    values = jnp.clip(jax.random.normal(key_vals, (TOKENS, F), jnp.float32), -6.0, 6.0)
    row_spread = math.log(4.0)
    order = jax.random.permutation(key_order, blocks)
    quiet_blocks = order[:quiet_count]
    heavy_block = order[quiet_count]
    block_of_row = jnp.arange(TOKENS, dtype=jnp.int32) // TOKENS_BLK
    quiet_row = jnp.any(block_of_row[:, None] == quiet_blocks[None, :], axis=1)
    heavy_index = heavy_block * TOKENS_BLK + jax.random.randint(key_heavy, (), 0, TOKENS_BLK)
    heavy_row = jnp.arange(TOKENS, dtype=jnp.int32) == heavy_index
    row_pos = jax.random.permutation(key_posit, TOKENS).astype(jnp.float32) / TOKENS
    col_pos = jnp.arange(F, dtype=jnp.float32) / F
    row_scale = jnp.exp(math.log(3.0) * row_pos + jax.random.uniform(key_rows, (TOKENS,), jnp.float32, 0.0, row_spread))
    row_scale = row_scale * jnp.where(heavy_row, 1.5, 1.0) * jnp.where(quiet_row, 0.1, 1.0)
    col_scale = jnp.exp(math.log(3.0) * col_pos + jax.random.uniform(key_cols, (F,), jnp.float32, 0.0, math.log(4.0)))
    base = 0.15 * values * row_scale[:, None] * col_scale[None, :]
    spike_rows = quiet_blocks * TOKENS_BLK + jax.random.randint(key_place, (quiet_count,), 0, TOKENS_BLK)
    spike_cols = jax.random.randint(key_where, (quiet_count,), 0, F)
    spike_signs = jnp.where(jax.random.randint(key_signs, (quiet_count,), 0, 2) == 0, -216.0, 216.0).astype(jnp.float32)
    base = base.at[spike_rows, spike_cols].set(spike_signs)
    return base.astype(jnp.bfloat16)


def block_scale(stream_key, shape, cuts, low, top_value):
    factor_of, own = 1.0, jax.random.fold_in(stream_key, 6)
    for axis_at, shards_of in cuts:
        heights = jnp.exp(jax.random.uniform(jax.random.fold_in(own, axis_at), (shards_of,), jnp.float32, low / len(cuts), top_value / len(cuts)))
        factor_of = factor_of * jnp.repeat(heights, shape[axis_at] // shards_of).reshape([-1 if axis == axis_at else 1 for axis in range(len(shape))])
    return factor_of


def bell_draw(own_key, dims, scale, reach, pieces=(), kind=jnp.bfloat16):
    entries = scale * jax.random.normal(own_key, dims, jnp.float32)
    if pieces:
        entries = entries * block_scale(own_key, dims, pieces, -0.22, 0.18)
    return jnp.clip(entries, -reach, reach).astype(kind)


def setup_inputs(seed: int = 0, part: int = 0) -> dict:
    seeds = jax.random.split(jax.random.key(seed), 4)
    part_keys = jax.random.split(jax.random.fold_in(seeds[3], part), 4)
    hidden_acts = draw_hidden_acts(jax.random.fold_in(jax.random.fold_in(seeds[3], part), 71), part)
    down_weight = bell_draw(seeds[1], (F, D), F ** -0.5, 0.0390625, ((0, 8), (1, 2)))
    amax_history = jnp.clip(jnp.exp(jax.random.uniform(part_keys[2], (HIST,), jnp.float32, math.log(3.0), math.log(12.0))), 3.0, 12.0)
    return {"hidden_acts": hidden_acts, "down_weight": down_weight, "amax_history": amax_history}


clip_ratio = 0.5
format_limit = 448.0


def reference(hidden_acts, down_weight, amax_history):
    peak_tok = jnp.max(jnp.abs(hidden_acts), axis=1).astype(jnp.float32)
    token_scale = clip_ratio * (peak_tok + 1e-6) / format_limit
    quantized = jnp.clip(hidden_acts.astype(jnp.float32) / token_scale[:, None], -format_limit, format_limit).astype(jnp.bfloat16)
    blocks = F // F_BLK
    quant_blocks = jnp.transpose(quantized.reshape(TOKENS, blocks, F_BLK), (1, 0, 2))
    weight_blocks = down_weight.reshape(blocks, F_BLK, D)

    def add_block(total, pair):
        quant_part, weight_part = pair
        partial_value = jnp.dot(quant_part, weight_part, preferred_element_type=jnp.float32)
        return total + partial_value, None

    summed, _ = lax.scan(add_block, jnp.zeros((TOKENS, D), jnp.float32), (quant_blocks, weight_blocks))
    result = summed * token_scale[:, None]
    previous = jnp.max(amax_history)
    scaled_out = jnp.clip(result / previous, -1.0, 1.0).astype(jnp.bfloat16)
    newest = jnp.max(jnp.abs(result))
    history_next = jnp.concatenate([newest[None], amax_history[:-1]])
    return scaled_out, token_scale, history_next
```

```python
import functools

import jax
import jax.numpy as jnp
from jax import lax
from jax.experimental import pallas as pl
from jax.experimental.pallas import tpu as pltpu
from jax.sharding import PartitionSpec as P

clip_ratio = 0.5
format_limit = 448.0
LANES = 128
CHUNK = 512
LAG = 2
MESH = pl.DeviceIdType.MESH
F32 = jnp.float32
BF16 = jnp.bfloat16


def kernel(
    n_row, n_col,
    h_ref, w_ref, hist_ref,
    out_ref, scale_ref, hist_out,
    hq, xq, lim, wv, pk, prec, ysend, yrecv, own, zsend, zrecv, mx, mrec,
    h_sem, hr_sem, w_sem, pk_send, pk_recv, y_sem, z_send, z_recv, m_send, m_recv,
):
    rows, depth = h_ref.shape
    groups = rows // LANES
    chunks = wv.shape[0]
    n_z = n_col // 2
    half = rows * n_row // 2
    block = rows * n_row // n_col
    peers = n_row * n_col
    r, c = lax.axis_index("row"), lax.axis_index("col")
    z, y = c // 2, lax.rem(c, 2)
    me = r * n_col + c
    my_rows = pl.ds(pl.multiple_of(r * rows, LANES), rows)

    def place(p):
        return {"row": p // n_col, "col": lax.rem(p, n_col)}

    def each_peer(do):
        def body(o, carry):
            do(o - 1, lax.rem(me + o, peers))
            return carry
        lax.fori_loop(1, peers, body, 0)

    barrier = pltpu.get_barrier_semaphore()
    each_peer(lambda i, p: pl.semaphore_signal(
        barrier, inc=1, device_id=place(p), device_id_type=MESH))

    own_copy = pltpu.make_async_copy(h_ref, hq.at[my_rows], h_sem)
    own_copy.start()

    def weight_copy(k):
        cols = pl.ds(pl.multiple_of(k * CHUNK, CHUNK), CHUNK)
        return pltpu.make_async_copy(w_ref.at[:, cols], wv.at[k], w_sem.at[k])

    for k in range(chunks):
        weight_copy(k).start()

    own_copy.wait()
    whole = depth // LANES
    for g in range(groups):
        at = pl.ds(pl.multiple_of(r * rows + g * LANES, LANES), LANES)
        m = jnp.abs(hq[at, 0:LANES])
        for j in range(1, whole):
            m = jnp.maximum(m, jnp.abs(hq[at, j * LANES:(j + 1) * LANES]))
        m = m.astype(F32)
        if depth % LANES:
            tail = jnp.abs(hq[at, whole * LANES:].astype(F32))
            m = jnp.maximum(m, jnp.max(tail, axis=1, keepdims=True))
        peak = jnp.max(jnp.transpose(m), axis=0, keepdims=True)
        pk[g:g + 1, :] = peak
        prec[me, g:g + 1, :] = peak

    pl.semaphore_wait(barrier, peers - 1)

    def peak_copy(i, p, slot):
        return pltpu.make_async_remote_copy(
            src_ref=pk, dst_ref=prec.at[slot], send_sem=pk_send.at[i],
            recv_sem=pk_recv.at[slot], device_id=place(p), device_id_type=MESH)

    each_peer(lambda i, p: peak_copy(i, p, me).start())
    acts_copies = []
    for o in range(1, n_row):
        to = lax.rem(r + o, n_row)
        acts_copies.append(pltpu.make_async_remote_copy(
            src_ref=hq.at[my_rows], dst_ref=hq.at[my_rows], send_sem=hr_sem.at[0, o - 1],
            recv_sem=hr_sem.at[1, o - 1], device_id={"row": to}, device_id_type=MESH))
    for copy in acts_copies:
        copy.start()

    each_peer(lambda i, p: peak_copy(i, p, p).wait_recv())
    for q in range(n_row):
        top = jnp.max(prec[q * n_col:(q + 1) * n_col], axis=0)
        for g in range(groups):
            edge = clip_ratio * (top[g:g + 1] + 1e-06)
            wide = jnp.transpose(jnp.broadcast_to(edge, (LANES, LANES)))
            at = q * rows + g * LANES
            lim[at:at + LANES, :] = wide.astype(BF16)
    mine = jnp.max(prec[pl.ds(r * n_col, n_col)], axis=0)
    scale_ref[...] = clip_ratio * (mine + 1e-06) / format_limit

    for copy in acts_copies:
        copy.wait_recv()

    def clip_block(b, carry):
        zt, side = b // 2, lax.rem(b, 2)
        col_at = 2 * zt + jnp.where(side == 0, 1 - y, y)
        src = pl.ds(pl.multiple_of(col_at * block, block), block)
        dst = pl.ds(pl.multiple_of(side * half + zt * block, block), block)
        edge = lim[src, :]
        for j in range(pl.cdiv(depth, LANES)):
            lo, hi = j * LANES, min((j + 1) * LANES, depth)
            e = edge[:, :hi - lo]
            xq[dst, lo:hi] = jnp.minimum(jnp.maximum(hq[src, lo:hi], -e), e)
        return carry

    lax.fori_loop(0, n_col, clip_block, 0)

    previous = hist_ref[0]
    for i in range(1, hist_ref.shape[0]):
        previous = jnp.maximum(previous, hist_ref[i])
    mx[...] = jnp.zeros_like(mx)

    def y_copy(k):
        return pltpu.make_async_remote_copy(
            src_ref=ysend.at[k], dst_ref=yrecv.at[k], send_sem=y_sem.at[0, k],
            recv_sem=y_sem.at[1, k], device_id={"col": 2 * z + 1 - y}, device_id_type=MESH)

    def z_copy(k, d):
        zt = lax.rem(z + d, n_z)
        src = pl.ds(pl.multiple_of(zt * block, block), block)
        return pltpu.make_async_remote_copy(
            src_ref=zsend.at[k, src], dst_ref=zrecv.at[k, d - 1], send_sem=z_send.at[k, d - 1],
            recv_sem=z_recv.at[k, d - 1], device_id={"col": 2 * zt + y}, device_id_type=MESH)

    def multiply(k):
        weight_copy(k).wait()
        p = jnp.dot(xq[...], wv[k], preferred_element_type=F32)
        ysend[k] = p[:half].astype(BF16)
        own[k] = p[half:]
        y_copy(k).start()

    def add_y(k):
        y_copy(k).wait_recv()
        s = own[k] + yrecv[k].astype(F32)
        own[k] = s
        zsend[k] = s.astype(BF16)
        for d in range(1, n_z):
            z_copy(k, d).start()

    def add_z(k):
        s = own[k, pl.ds(pl.multiple_of(z * block, block), block)]
        for d in range(1, n_z):
            z_copy(k, d).wait_recv()
            s = s + zrecv[k, d - 1].astype(F32)
        m = jnp.max(jnp.abs(s), axis=0, keepdims=True)
        for j in range(CHUNK // LANES):
            mx[...] = jnp.maximum(mx[...], m[:, j * LANES:(j + 1) * LANES])
        cols = pl.ds(pl.multiple_of(k * CHUNK, CHUNK), CHUNK)
        out_ref[:, cols] = jnp.clip(s / previous, -1.0, 1.0).astype(BF16)

    def step(k, carry):
        pl.when(k < chunks)(lambda: multiply(k))
        pl.when(jnp.logical_and(k >= LAG, k < chunks + LAG))(lambda: add_y(k - LAG))
        pl.when(k >= 2 * LAG)(lambda: add_z(k - 2 * LAG))
        return carry

    lax.fori_loop(0, chunks + 2 * LAG, step, 0)

    mrec[me] = mx[...]

    def max_copy(i, p, slot):
        return pltpu.make_async_remote_copy(
            src_ref=mx, dst_ref=mrec.at[slot], send_sem=m_send.at[i],
            recv_sem=m_recv.at[slot], device_id=place(p), device_id_type=MESH)

    each_peer(lambda i, p: max_copy(i, p, me).start())

    def sent(k, carry):
        y_copy(k).wait_send()
        for d in range(1, n_z):
            z_copy(k, d).wait_send()
        return carry

    lax.fori_loop(0, chunks, sent, 0)
    each_peer(lambda i, p: peak_copy(i, p, me).wait_send())
    for copy in acts_copies:
        copy.wait_send()
    each_peer(lambda i, p: max_copy(i, p, p).wait_recv())
    hist_out[0] = jnp.max(mrec[...])
    for i in range(1, hist_ref.shape[0]):
        hist_out[i] = hist_ref[i - 1]
    each_peer(lambda i, p: max_copy(i, p, me).wait_send())


def on_device(n_row, n_col, hidden_acts, down_weight, amax_history):
    rows, depth = hidden_acts.shape
    width = down_weight.shape[1]
    groups = rows // LANES
    tokens = rows * n_row
    half, block, chunks, n_z = tokens // 2, tokens // n_col, width // CHUNK, n_col // 2
    peers = n_row * n_col
    dma = pltpu.SemaphoreType.DMA
    vmem = pl.BlockSpec(memory_space=pltpu.VMEM)
    smem = pl.BlockSpec(memory_space=pltpu.SMEM)
    anywhere = pl.BlockSpec(memory_space=pl.ANY)
    scaled_out, scale, history = pl.pallas_call(
        functools.partial(kernel, n_row, n_col),
        out_shape=(
            jax.ShapeDtypeStruct((block, width), BF16),
            jax.ShapeDtypeStruct((groups, LANES), F32),
            jax.ShapeDtypeStruct(amax_history.shape, F32),
        ),
        in_specs=[anywhere, anywhere, smem],
        out_specs=(vmem, vmem, smem),
        scratch_shapes=[
            pltpu.VMEM((tokens, depth), BF16),
            pltpu.VMEM((tokens, depth), BF16),
            pltpu.VMEM((tokens, LANES), BF16),
            pltpu.VMEM((chunks, depth, CHUNK), BF16),
            pltpu.VMEM((groups, LANES), F32),
            pltpu.VMEM((peers, groups, LANES), F32),
            pltpu.VMEM((chunks, half, CHUNK), BF16),
            pltpu.VMEM((chunks, half, CHUNK), BF16),
            pltpu.VMEM((chunks, half, CHUNK), F32),
            pltpu.VMEM((chunks, half, CHUNK), BF16),
            pltpu.VMEM((chunks, n_z - 1, block, CHUNK), BF16),
            pltpu.VMEM((1, LANES), F32),
            pltpu.VMEM((peers, 1, LANES), F32),
            dma, dma((2, n_row - 1)), dma((chunks,)), dma((peers,)), dma((peers,)),
            dma((2, chunks)), dma((chunks, n_z - 1)), dma((chunks, n_z - 1)),
            dma((peers,)), dma((peers,)),
        ],
        compiler_params=pltpu.CompilerParams(
            collective_id=0, has_side_effects=True, vmem_limit_bytes=56 << 20),
        cost_estimate=pl.CostEstimate(
            flops=2 * tokens * depth * width, bytes_accessed=2 * depth * width, transcendentals=0),
    )(hidden_acts, down_weight, amax_history)
    return scaled_out, scale.reshape(rows), history


def solution(mesh):
    in_specs = (P(("grp", "row"), "col"), P("col", "row"), P("grp"))
    out_specs = (P(("grp", "col"), "row"), P(("grp", "row")), P("grp"))
    return jax.shard_map(
        functools.partial(on_device, mesh.shape["row"], mesh.shape["col"]),
        mesh=mesh, in_specs=in_specs, out_specs=out_specs, check_vma=False)
```

```python
import functools

import jax
import jax.numpy as jnp
from jax import lax
from jax.experimental import pallas as pl
from jax.experimental.pallas import tpu as pltpu
from jax.sharding import PartitionSpec as P

clip_ratio = 0.5
format_limit = 448.0
LANES = 128
CHUNK = 256
LAG = 3
EARLY = 4
MESH = pl.DeviceIdType.MESH
F32 = jnp.float32
BF16 = jnp.bfloat16


def kernel(
    n_row, n_col,
    h_ref, w_ref, hist_ref,
    out_ref, scale_ref, hist_out,
    hq, xq, lim, wv, pk, prec, ysend, yrecv, own, zsend, zrecv, mx, mrec,
    h_sem, hr_sem, w_sem, pk_send, pk_recv, y_sem, z_send, z_recv, m_send, m_recv,
):
    rows, depth = h_ref.shape
    groups = rows // LANES
    chunks = wv.shape[0]
    n_z = n_col // 2
    half = rows * n_row // 2
    block = rows * n_row // n_col
    peers = n_row * n_col
    r, c = lax.axis_index("row"), lax.axis_index("col")
    z, y = c // 2, lax.rem(c, 2)
    me = r * n_col + c
    my_rows = pl.ds(pl.multiple_of(r * rows, LANES), rows)

    def place(p):
        return {"row": p // n_col, "col": lax.rem(p, n_col)}

    def each_peer(do):
        def body(o, carry):
            do(o - 1, lax.rem(me + o, peers))
            return carry
        lax.fori_loop(1, peers, body, 0)

    barrier = pltpu.get_barrier_semaphore()
    each_peer(lambda i, p: pl.semaphore_signal(
        barrier, inc=1, device_id=place(p), device_id_type=MESH))

    own_copy = pltpu.make_async_copy(h_ref, hq.at[my_rows], h_sem)
    own_copy.start()

    def weight_copy(k):
        cols = pl.ds(pl.multiple_of(k * CHUNK, CHUNK), CHUNK)
        return pltpu.make_async_copy(w_ref.at[:, cols], wv.at[k], w_sem.at[k])

    for k in range(EARLY):
        weight_copy(k).start()

    own_copy.wait()
    whole = depth // LANES
    for g in range(groups):
        at = pl.ds(pl.multiple_of(r * rows + g * LANES, LANES), LANES)
        m = jnp.abs(hq[at, 0:LANES])
        for j in range(1, whole):
            m = jnp.maximum(m, jnp.abs(hq[at, j * LANES:(j + 1) * LANES]))
        m = m.astype(F32)
        if depth % LANES:
            tail = jnp.abs(hq[at, whole * LANES:].astype(F32))
            m = jnp.maximum(m, jnp.max(tail, axis=1, keepdims=True))
        peak = jnp.max(jnp.transpose(m), axis=0, keepdims=True)
        pk[g:g + 1, :] = peak
        prec[me, g:g + 1, :] = peak

    pl.semaphore_wait(barrier, peers - 1)

    def peak_copy(i, p, slot):
        return pltpu.make_async_remote_copy(
            src_ref=pk, dst_ref=prec.at[slot], send_sem=pk_send.at[i],
            recv_sem=pk_recv.at[slot], device_id=place(p), device_id_type=MESH)

    each_peer(lambda i, p: peak_copy(i, p, me).start())
    acts_copies = []
    for o in range(1, n_row):
        to = lax.rem(r + o, n_row)
        acts_copies.append(pltpu.make_async_remote_copy(
            src_ref=hq.at[my_rows], dst_ref=hq.at[my_rows], send_sem=hr_sem.at[0, o - 1],
            recv_sem=hr_sem.at[1, o - 1], device_id={"row": to}, device_id_type=MESH))
    for copy in acts_copies:
        copy.start()
    for k in range(EARLY, chunks):
        weight_copy(k).start()

    each_peer(lambda i, p: peak_copy(i, p, p).wait_recv())
    for q in range(n_row):
        top = jnp.max(prec[q * n_col:(q + 1) * n_col], axis=0)
        for g in range(groups):
            edge = clip_ratio * (top[g:g + 1] + 1e-06)
            wide = jnp.transpose(jnp.broadcast_to(edge, (LANES, LANES)))
            at = q * rows + g * LANES
            lim[at:at + LANES, :] = wide.astype(BF16)
    mine = jnp.max(prec[pl.ds(r * n_col, n_col)], axis=0)
    scale_ref[...] = clip_ratio * (mine + 1e-06) / format_limit

    for copy in acts_copies:
        copy.wait_recv()

    def clip_block(b, carry):
        zt, side = b // 2, lax.rem(b, 2)
        col_at = 2 * zt + jnp.where(side == 0, 1 - y, y)
        src = pl.ds(pl.multiple_of(col_at * block, block), block)
        dst = pl.ds(pl.multiple_of(side * half + zt * block, block), block)
        edge = lim[src, :]
        for j in range(pl.cdiv(depth, LANES)):
            lo, hi = j * LANES, min((j + 1) * LANES, depth)
            e = edge[:, :hi - lo]
            xq[dst, lo:hi] = jnp.minimum(jnp.maximum(hq[src, lo:hi], -e), e)
        return carry

    lax.fori_loop(0, n_col, clip_block, 0)

    previous = hist_ref[0]
    for i in range(1, hist_ref.shape[0]):
        previous = jnp.maximum(previous, hist_ref[i])
    mx[...] = jnp.zeros_like(mx)

    def y_copy(k):
        return pltpu.make_async_remote_copy(
            src_ref=ysend.at[k], dst_ref=yrecv.at[k], send_sem=y_sem.at[0, k],
            recv_sem=y_sem.at[1, k], device_id={"col": 2 * z + 1 - y}, device_id_type=MESH)

    def z_copy(k, d):
        zt = lax.rem(z + d, n_z)
        src = pl.ds(pl.multiple_of(zt * block, block), block)
        return pltpu.make_async_remote_copy(
            src_ref=zsend.at[k, src], dst_ref=zrecv.at[k, d - 1], send_sem=z_send.at[k, d - 1],
            recv_sem=z_recv.at[k, d - 1], device_id={"col": 2 * zt + y}, device_id_type=MESH)

    def multiply(k):
        weight_copy(k).wait()
        p = jnp.dot(xq[...], wv[k], preferred_element_type=F32)
        ysend[k] = p[:half].astype(BF16)
        own[k] = p[half:]
        y_copy(k).start()

    def add_y(k):
        y_copy(k).wait_recv()
        s = own[k] + yrecv[k].astype(F32)
        own[k] = s
        zsend[k] = s.astype(BF16)
        for d in range(1, n_z):
            z_copy(k, d).start()

    def add_z(k):
        s = own[k, pl.ds(pl.multiple_of(z * block, block), block)]
        for d in range(1, n_z):
            z_copy(k, d).wait_recv()
            s = s + zrecv[k, d - 1].astype(F32)
        m = jnp.max(jnp.abs(s), axis=0, keepdims=True)
        for j in range(CHUNK // LANES):
            mx[...] = jnp.maximum(mx[...], m[:, j * LANES:(j + 1) * LANES])
        cols = pl.ds(pl.multiple_of(k * CHUNK, CHUNK), CHUNK)
        out_ref[:, cols] = jnp.clip(s / previous, -1.0, 1.0).astype(BF16)

    def step(k, carry):
        pl.when(k < chunks)(lambda: multiply(k))
        pl.when(jnp.logical_and(k >= LAG, k < chunks + LAG))(lambda: add_y(k - LAG))
        pl.when(k >= 2 * LAG)(lambda: add_z(k - 2 * LAG))
        return carry

    lax.fori_loop(0, chunks + 2 * LAG, step, 0)

    mrec[me] = mx[...]

    def max_copy(i, p, slot):
        return pltpu.make_async_remote_copy(
            src_ref=mx, dst_ref=mrec.at[slot], send_sem=m_send.at[i],
            recv_sem=m_recv.at[slot], device_id=place(p), device_id_type=MESH)

    each_peer(lambda i, p: max_copy(i, p, me).start())

    def sent(k, carry):
        y_copy(k).wait_send()
        for d in range(1, n_z):
            z_copy(k, d).wait_send()
        return carry

    lax.fori_loop(0, chunks, sent, 0)
    each_peer(lambda i, p: peak_copy(i, p, me).wait_send())
    for copy in acts_copies:
        copy.wait_send()
    each_peer(lambda i, p: max_copy(i, p, p).wait_recv())
    hist_out[0] = jnp.max(mrec[...])
    for i in range(1, hist_ref.shape[0]):
        hist_out[i] = hist_ref[i - 1]
    each_peer(lambda i, p: max_copy(i, p, me).wait_send())


def write_out(a_ref, b_ref, c_ref, a_out, b_out, c_out):
    a_out[...] = a_ref[...]
    b_out[...] = b_ref[...]
    for i in range(c_ref.shape[0]):
        c_out[i] = c_ref[i]


def on_device(n_row, n_col, hidden_acts, down_weight, amax_history):
    rows, depth = hidden_acts.shape
    width = down_weight.shape[1]
    groups = rows // LANES
    tokens = rows * n_row
    half, block, chunks, n_z = tokens // 2, tokens // n_col, width // CHUNK, n_col // 2
    peers = n_row * n_col
    dma = pltpu.SemaphoreType.DMA
    vmem = pl.BlockSpec(memory_space=pltpu.VMEM)
    smem = pl.BlockSpec(memory_space=pltpu.SMEM)
    anywhere = pl.BlockSpec(memory_space=pl.ANY)
    out_shape = (
        jax.ShapeDtypeStruct((block, width), BF16),
        jax.ShapeDtypeStruct((groups, LANES), F32),
        jax.ShapeDtypeStruct(amax_history.shape, F32),
    )
    results = pl.pallas_call(
        functools.partial(kernel, n_row, n_col),
        out_shape=out_shape,
        in_specs=[anywhere, anywhere, smem],
        out_specs=(vmem, vmem, smem),
        scratch_shapes=[
            pltpu.VMEM((tokens, depth), BF16),
            pltpu.VMEM((tokens, depth), BF16),
            pltpu.VMEM((tokens, LANES), BF16),
            pltpu.VMEM((chunks, depth, CHUNK), BF16),
            pltpu.VMEM((groups, LANES), F32),
            pltpu.VMEM((peers, groups, LANES), F32),
            pltpu.VMEM((chunks, half, CHUNK), BF16),
            pltpu.VMEM((chunks, half, CHUNK), BF16),
            pltpu.VMEM((chunks, half, CHUNK), F32),
            pltpu.VMEM((chunks, half, CHUNK), BF16),
            pltpu.VMEM((chunks, n_z - 1, block, CHUNK), BF16),
            pltpu.VMEM((1, LANES), F32),
            pltpu.VMEM((peers, 1, LANES), F32),
            dma, dma((2, n_row - 1)), dma((chunks,)), dma((peers,)), dma((peers,)),
            dma((2, chunks)), dma((chunks, n_z - 1)), dma((chunks, n_z - 1)),
            dma((peers,)), dma((peers,)),
        ],
        compiler_params=pltpu.CompilerParams(
            collective_id=0, has_side_effects=True, vmem_limit_bytes=56 << 20),
        cost_estimate=pl.CostEstimate(
            flops=2 * tokens * depth * width, bytes_accessed=2 * depth * width, transcendentals=0),
    )(hidden_acts, down_weight, amax_history)
    scaled_out, scale, history = pl.pallas_call(
        write_out, out_shape=out_shape, in_specs=[vmem, vmem, smem], out_specs=(vmem, vmem, smem),
        compiler_params=pltpu.CompilerParams(vmem_limit_bytes=60 << 20),
    )(*results)
    return scaled_out, scale.reshape(rows), history


def solution(mesh):
    in_specs = (P(("grp", "row"), "col"), P("col", "row"), P("grp"))
    out_specs = (P(("grp", "col"), "row"), P(("grp", "row")), P("grp"))
    return jax.shard_map(
        functools.partial(on_device, mesh.shape["row"], mesh.shape["col"]),
        mesh=mesh, in_specs=in_specs, out_specs=out_specs, check_vma=False)
```

```python
import functools

import jax
import jax.numpy as jnp
from jax import lax
from jax.experimental import pallas as pl
from jax.experimental.pallas import tpu as pltpu
from jax.sharding import PartitionSpec as P

clip_ratio = 0.5
format_limit = 448.0
LANES = 128
CHUNK = 256
LAG = 3
EARLY = 4
MESH = pl.DeviceIdType.MESH
F32 = jnp.float32
BF16 = jnp.bfloat16


def kernel(
    n_row, n_col,
    h_ref, w_ref, hist_ref,
    out_ref, scale_ref, hist_out,
    hq, xq, lim, wv, pk, prec, send1, recv1, own, send2, recv2, send3, recv3, mx, mrec,
    h_sem, hr_sem, w_sem, pk_send, pk_recv, s1_sem, s2_sem, s3_send, s3_recv, m_send, m_recv,
):
    rows, depth = h_ref.shape
    groups = rows // LANES
    chunks = wv.shape[0]
    n_far = n_col // 4
    half = rows * n_row // 2
    quarter = half // 2
    block = rows * n_row // n_col
    peers = n_row * n_col
    r, c = lax.axis_index("row"), lax.axis_index("col")
    far, near, y = c // 4, lax.rem(c // 2, 2), lax.rem(c, 2)
    me = r * n_col + c
    my_rows = pl.ds(pl.multiple_of(r * rows, LANES), rows)

    def place(p):
        return {"row": p // n_col, "col": lax.rem(p, n_col)}

    def each_peer(do):
        def body(o, carry):
            do(o - 1, lax.rem(me + o, peers))
            return carry
        lax.fori_loop(1, peers, body, 0)

    barrier = pltpu.get_barrier_semaphore()
    each_peer(lambda i, p: pl.semaphore_signal(
        barrier, inc=1, device_id=place(p), device_id_type=MESH))

    own_copy = pltpu.make_async_copy(h_ref, hq.at[my_rows], h_sem)
    own_copy.start()

    def weight_copy(k):
        cols = pl.ds(pl.multiple_of(k * CHUNK, CHUNK), CHUNK)
        return pltpu.make_async_copy(w_ref.at[:, cols], wv.at[k], w_sem.at[k])

    for k in range(EARLY):
        weight_copy(k).start()

    own_copy.wait()
    whole = depth // LANES
    for g in range(groups):
        at = pl.ds(pl.multiple_of(r * rows + g * LANES, LANES), LANES)
        m = jnp.abs(hq[at, 0:LANES])
        for j in range(1, whole):
            m = jnp.maximum(m, jnp.abs(hq[at, j * LANES:(j + 1) * LANES]))
        m = m.astype(F32)
        if depth % LANES:
            tail = jnp.abs(hq[at, whole * LANES:].astype(F32))
            m = jnp.maximum(m, jnp.max(tail, axis=1, keepdims=True))
        peak = jnp.max(jnp.transpose(m), axis=0, keepdims=True)
        pk[g:g + 1, :] = peak
        prec[me, g:g + 1, :] = peak

    pl.semaphore_wait(barrier, peers - 1)

    def peak_copy(i, p, slot):
        return pltpu.make_async_remote_copy(
            src_ref=pk, dst_ref=prec.at[slot], send_sem=pk_send.at[i],
            recv_sem=pk_recv.at[slot], device_id=place(p), device_id_type=MESH)

    each_peer(lambda i, p: peak_copy(i, p, me).start())
    acts_copies = []
    for o in range(1, n_row):
        to = lax.rem(r + o, n_row)
        acts_copies.append(pltpu.make_async_remote_copy(
            src_ref=hq.at[my_rows], dst_ref=hq.at[my_rows], send_sem=hr_sem.at[0, o - 1],
            recv_sem=hr_sem.at[1, o - 1], device_id={"row": to}, device_id_type=MESH))
    for copy in acts_copies:
        copy.start()
    for k in range(EARLY, chunks):
        weight_copy(k).start()

    each_peer(lambda i, p: peak_copy(i, p, p).wait_recv())
    for q in range(n_row):
        top = jnp.max(prec[q * n_col:(q + 1) * n_col], axis=0)
        for g in range(groups):
            edge = clip_ratio * (top[g:g + 1] + 1e-06)
            wide = jnp.transpose(jnp.broadcast_to(edge, (LANES, LANES)))
            at = q * rows + g * LANES
            lim[at:at + LANES, :] = wide.astype(BF16)
    mine = jnp.max(prec[pl.ds(r * n_col, n_col)], axis=0)
    scale_ref[...] = clip_ratio * (mine + 1e-06) / format_limit

    for copy in acts_copies:
        copy.wait_recv()

    def clip_block(b, carry):
        part, d = b // n_far, lax.rem(b, n_far)
        to_y = lax.rem(y + 1 - part // 2, 2)
        to_near = lax.rem(near + 1 - lax.rem(part, 2), 2)
        col_at = 4 * lax.rem(far + d, n_far) + 2 * to_near + to_y
        src = pl.ds(pl.multiple_of(col_at * block, block), block)
        dst = pl.ds(pl.multiple_of(b * block, block), block)
        edge = lim[src, :]
        for j in range(pl.cdiv(depth, LANES)):
            lo, hi = j * LANES, min((j + 1) * LANES, depth)
            e = edge[:, :hi - lo]
            xq[dst, lo:hi] = jnp.minimum(jnp.maximum(hq[src, lo:hi], -e), e)
        return carry

    lax.fori_loop(0, n_col, clip_block, 0)

    previous = hist_ref[0]
    for i in range(1, hist_ref.shape[0]):
        previous = jnp.maximum(previous, hist_ref[i])
    mx[...] = jnp.zeros_like(mx)

    y_peer = 4 * far + 2 * near + 1 - y
    near_peer = 4 * far + 2 * (1 - near) + y

    def near_first(k):
        return lax.rem(k, 4) == 1

    def copy1(k):
        return pltpu.make_async_remote_copy(
            src_ref=send1.at[k], dst_ref=recv1.at[k], send_sem=s1_sem.at[0, k],
            recv_sem=s1_sem.at[1, k], device_id_type=MESH,
            device_id={"col": jnp.where(near_first(k), near_peer, y_peer)})

    def copy2(k):
        return pltpu.make_async_remote_copy(
            src_ref=send2.at[k], dst_ref=recv2.at[k], send_sem=s2_sem.at[0, k],
            recv_sem=s2_sem.at[1, k], device_id_type=MESH,
            device_id={"col": jnp.where(near_first(k), y_peer, near_peer)})

    def copy3(k, d):
        to = 4 * lax.rem(far + d, n_far) + 2 * near + y
        return pltpu.make_async_remote_copy(
            src_ref=send3.at[k, d - 1], dst_ref=recv3.at[k, d - 1],
            send_sem=s3_send.at[k, d - 1], recv_sem=s3_recv.at[k, d - 1],
            device_id={"col": to}, device_id_type=MESH)

    def multiply(k):
        weight_copy(k).wait()
        p = jnp.dot(xq[...], wv[k], preferred_element_type=F32)
        p1, p2 = p[quarter:half], p[half:half + quarter]
        swap = near_first(k)
        send1[k, :quarter] = p[:quarter].astype(BF16)
        send1[k, quarter:] = jnp.where(swap, p2, p1).astype(BF16)
        copy1(k).start()
        own[k, :quarter] = jnp.where(swap, p1, p2)
        own[k, quarter:] = p[half + quarter:]

    def add1(k):
        copy1(k).wait_recv()
        send2[k] = (own[k, :quarter] + recv1[k, :quarter].astype(F32)).astype(BF16)
        copy2(k).start()
        own[k, quarter:] = own[k, quarter:] + recv1[k, quarter:].astype(F32)

    def add2(k):
        copy2(k).wait_recv()
        s = own[k, quarter:] + recv2[k].astype(F32)
        for d in range(1, n_far):
            send3[k, d - 1] = s[d * block:(d + 1) * block].astype(BF16)
            copy3(k, d).start()
        own[k, :block] = s[:block]

    def add3(k):
        s = own[k, :block]
        for d in range(1, n_far):
            copy3(k, d).wait_recv()
            s = s + recv3[k, d - 1].astype(F32)
        m = jnp.max(jnp.abs(s), axis=0, keepdims=True)
        for j in range(CHUNK // LANES):
            mx[...] = jnp.maximum(mx[...], m[:, j * LANES:(j + 1) * LANES])
        cols = pl.ds(pl.multiple_of(k * CHUNK, CHUNK), CHUNK)
        out_ref[:, cols] = jnp.clip(s / previous, -1.0, 1.0).astype(BF16)

    def step(k, carry):
        def at(lag, do):
            pl.when(jnp.logical_and(k >= lag, k < chunks + lag))(lambda: do(k - lag))
        at(0, multiply)
        at(LAG, add1)
        at(2 * LAG, add2)
        at(3 * LAG, add3)
        return carry

    lax.fori_loop(0, chunks + 3 * LAG, step, 0)

    mrec[me] = mx[...]

    def max_copy(i, p, slot):
        return pltpu.make_async_remote_copy(
            src_ref=mx, dst_ref=mrec.at[slot], send_sem=m_send.at[i],
            recv_sem=m_recv.at[slot], device_id=place(p), device_id_type=MESH)

    each_peer(lambda i, p: max_copy(i, p, me).start())

    def sent(k, carry):
        copy1(k).wait_send()
        copy2(k).wait_send()
        for d in range(1, n_far):
            copy3(k, d).wait_send()
        return carry

    lax.fori_loop(0, chunks, sent, 0)
    each_peer(lambda i, p: peak_copy(i, p, me).wait_send())
    for copy in acts_copies:
        copy.wait_send()
    each_peer(lambda i, p: max_copy(i, p, p).wait_recv())
    hist_out[0] = jnp.max(mrec[...])
    for i in range(1, hist_ref.shape[0]):
        hist_out[i] = hist_ref[i - 1]
    each_peer(lambda i, p: max_copy(i, p, me).wait_send())


def write_out(a_ref, b_ref, c_ref, a_out, b_out, c_out):
    a_out[...] = a_ref[...]
    b_out[...] = b_ref[...]
    for i in range(c_ref.shape[0]):
        c_out[i] = c_ref[i]


def on_device(n_row, n_col, hidden_acts, down_weight, amax_history):
    rows, depth = hidden_acts.shape
    width = down_weight.shape[1]
    groups = rows // LANES
    tokens = rows * n_row
    half, block, chunks, n_far = tokens // 2, tokens // n_col, width // CHUNK, n_col // 4
    peers = n_row * n_col
    dma = pltpu.SemaphoreType.DMA
    vmem = pl.BlockSpec(memory_space=pltpu.VMEM)
    smem = pl.BlockSpec(memory_space=pltpu.SMEM)
    anywhere = pl.BlockSpec(memory_space=pl.ANY)
    out_shape = (
        jax.ShapeDtypeStruct((block, width), BF16),
        jax.ShapeDtypeStruct((groups, LANES), F32),
        jax.ShapeDtypeStruct(amax_history.shape, F32),
    )
    results = pl.pallas_call(
        functools.partial(kernel, n_row, n_col),
        out_shape=out_shape,
        in_specs=[anywhere, anywhere, smem],
        out_specs=(vmem, vmem, smem),
        scratch_shapes=[
            pltpu.VMEM((tokens, depth), BF16),
            pltpu.VMEM((tokens, depth), BF16),
            pltpu.VMEM((tokens, LANES), BF16),
            pltpu.VMEM((chunks, depth, CHUNK), BF16),
            pltpu.VMEM((groups, LANES), F32),
            pltpu.VMEM((peers, groups, LANES), F32),
            pltpu.VMEM((chunks, half, CHUNK), BF16),
            pltpu.VMEM((chunks, half, CHUNK), BF16),
            pltpu.VMEM((chunks, half, CHUNK), F32),
            pltpu.VMEM((chunks, half // 2, CHUNK), BF16),
            pltpu.VMEM((chunks, half // 2, CHUNK), BF16),
            pltpu.VMEM((chunks, n_far - 1, block, CHUNK), BF16),
            pltpu.VMEM((chunks, n_far - 1, block, CHUNK), BF16),
            pltpu.VMEM((1, LANES), F32),
            pltpu.VMEM((peers, 1, LANES), F32),
            dma, dma((2, n_row - 1)), dma((chunks,)), dma((peers,)), dma((peers,)),
            dma((2, chunks)), dma((2, chunks)), dma((chunks, n_far - 1)), dma((chunks, n_far - 1)),
            dma((peers,)), dma((peers,)),
        ],
        compiler_params=pltpu.CompilerParams(
            collective_id=0, has_side_effects=True, vmem_limit_bytes=56 << 20),
        cost_estimate=pl.CostEstimate(
            flops=2 * tokens * depth * width, bytes_accessed=2 * depth * width, transcendentals=0),
    )(hidden_acts, down_weight, amax_history)
    scaled_out, scale, history = pl.pallas_call(
        write_out, out_shape=out_shape, in_specs=[vmem, vmem, smem], out_specs=(vmem, vmem, smem),
        compiler_params=pltpu.CompilerParams(vmem_limit_bytes=60 << 20),
    )(*results)
    return scaled_out, scale.reshape(rows), history


def solution(mesh):
    in_specs = (P(("grp", "row"), "col"), P("col", "row"), P("grp"))
    out_specs = (P(("grp", "col"), "row"), P(("grp", "row")), P("grp"))
    return jax.shard_map(
        functools.partial(on_device, mesh.shape["row"], mesh.shape["col"]),
        mesh=mesh, in_specs=in_specs, out_specs=out_specs, check_vma=False)
```

```python
import functools

import jax
import jax.numpy as jnp
from jax import lax
from jax.experimental import pallas as pl
from jax.experimental.pallas import tpu as pltpu
from jax.sharding import PartitionSpec as P

clip_ratio = 0.5
format_limit = 448.0
LANES = 128
CHUNK = 256
LAG = 3
EARLY = 4
MESH = pl.DeviceIdType.MESH
F32 = jnp.float32
BF16 = jnp.bfloat16


def kernel(
    n_row, n_col,
    h_ref, w_ref, hist_ref,
    out_ref, scale_ref, hist_out,
    hq, xq, lim, wv, pk, prec, send1, recv1, own, send2, recv2, send3, recv3, mx, mrec,
    h_sem, hr_sem, w_sem, pk_send, pk_recv, s1_sem, s2_sem, s3_send, s3_recv, m_send, m_recv,
):
    rows, depth = h_ref.shape
    groups = rows // LANES
    chunks = wv.shape[0]
    n_far = n_col // 4
    half = rows * n_row // 2
    quarter = half // 2
    block = rows * n_row // n_col
    peers = n_row * n_col
    r, c = lax.axis_index("row"), lax.axis_index("col")
    far, near, y = c // 4, lax.rem(c // 2, 2), lax.rem(c, 2)
    me = r * n_col + c
    my_rows = pl.ds(pl.multiple_of(r * rows, LANES), rows)

    def place(p):
        return {"row": p // n_col, "col": lax.rem(p, n_col)}

    def each_peer(do):
        def body(o, carry):
            do(o - 1, lax.rem(me + o, peers))
            return carry
        lax.fori_loop(1, peers, body, 0)

    barrier = pltpu.get_barrier_semaphore()
    each_peer(lambda i, p: pl.semaphore_signal(
        barrier, inc=1, device_id=place(p), device_id_type=MESH))

    own_copy = pltpu.make_async_copy(h_ref, hq.at[my_rows], h_sem)
    own_copy.start()

    def weight_copy(k):
        cols = pl.ds(pl.multiple_of(k * CHUNK, CHUNK), CHUNK)
        return pltpu.make_async_copy(w_ref.at[:, cols], wv.at[k], w_sem.at[k])

    for k in range(EARLY):
        weight_copy(k).start()

    own_copy.wait()
    whole = depth // LANES
    for g in range(groups):
        at = pl.ds(pl.multiple_of(r * rows + g * LANES, LANES), LANES)
        m = jnp.abs(hq[at, 0:LANES])
        for j in range(1, whole):
            m = jnp.maximum(m, jnp.abs(hq[at, j * LANES:(j + 1) * LANES]))
        m = m.astype(F32)
        if depth % LANES:
            tail = jnp.abs(hq[at, whole * LANES:].astype(F32))
            m = jnp.maximum(m, jnp.max(tail, axis=1, keepdims=True))
        peak = jnp.max(jnp.transpose(m), axis=0, keepdims=True)
        pk[g:g + 1, :] = peak
        prec[me, g:g + 1, :] = peak

    pl.semaphore_wait(barrier, peers - 1)

    def peak_copy(i, p, slot):
        return pltpu.make_async_remote_copy(
            src_ref=pk, dst_ref=prec.at[slot], send_sem=pk_send.at[i],
            recv_sem=pk_recv.at[slot], device_id=place(p), device_id_type=MESH)

    each_peer(lambda i, p: peak_copy(i, p, me).start())
    acts_copies = []
    for o in range(1, n_row):
        to = lax.rem(r + o, n_row)
        acts_copies.append(pltpu.make_async_remote_copy(
            src_ref=hq.at[my_rows], dst_ref=hq.at[my_rows], send_sem=hr_sem.at[0, o - 1],
            recv_sem=hr_sem.at[1, o - 1], device_id={"row": to}, device_id_type=MESH))
    for copy in acts_copies:
        copy.start()
    for k in range(EARLY, chunks):
        weight_copy(k).start()

    each_peer(lambda i, p: peak_copy(i, p, p).wait_recv())
    for q in range(n_row):
        top = jnp.max(prec[q * n_col:(q + 1) * n_col], axis=0)
        for g in range(groups):
            edge = clip_ratio * (top[g:g + 1] + 1e-06)
            wide = jnp.transpose(jnp.broadcast_to(edge, (LANES, LANES)))
            at = q * rows + g * LANES
            lim[at:at + LANES, :] = wide.astype(BF16)
    mine = jnp.max(prec[pl.ds(r * n_col, n_col)], axis=0)
    scale_ref[...] = clip_ratio * (mine + 1e-06) / format_limit

    for copy in acts_copies:
        copy.wait_recv()

    def clip_block(b, carry):
        part, d = b // n_far, lax.rem(b, n_far)
        to_y = lax.rem(y + 1 - part // 2, 2)
        to_near = lax.rem(near + 1 - lax.rem(part, 2), 2)
        col_at = 4 * lax.rem(far + d, n_far) + 2 * to_near + to_y
        src = pl.ds(pl.multiple_of(col_at * block, block), block)
        dst = pl.ds(pl.multiple_of(b * block, block), block)
        edge = lim[src, :]
        for j in range(pl.cdiv(depth, LANES)):
            lo, hi = j * LANES, min((j + 1) * LANES, depth)
            e = edge[:, :hi - lo]
            xq[dst, lo:hi] = jnp.minimum(jnp.maximum(hq[src, lo:hi], -e), e)
        return carry

    lax.fori_loop(0, n_col, clip_block, 0)

    previous = hist_ref[0]
    for i in range(1, hist_ref.shape[0]):
        previous = jnp.maximum(previous, hist_ref[i])
    mx[...] = jnp.zeros_like(mx)

    y_peer = 4 * far + 2 * near + 1 - y
    near_peer = 4 * far + 2 * (1 - near) + y

    cut = (depth // 256 + 1) // 2 * 256

    def near_first(k):
        return lax.rem(k, 4) == 1

    def copy1(k):
        return pltpu.make_async_remote_copy(
            src_ref=send1.at[k], dst_ref=recv1.at[k], send_sem=s1_sem.at[0, k],
            recv_sem=s1_sem.at[1, k], device_id_type=MESH,
            device_id={"col": jnp.where(near_first(k), near_peer, y_peer)})

    def copy2(k):
        return pltpu.make_async_remote_copy(
            src_ref=send2.at[k], dst_ref=recv2.at[k], send_sem=s2_sem.at[0, k],
            recv_sem=s2_sem.at[1, k], device_id_type=MESH,
            device_id={"col": jnp.where(near_first(k), y_peer, near_peer)})

    def copy3(k, d):
        to = 4 * lax.rem(far + d, n_far) + 2 * near + y
        return pltpu.make_async_remote_copy(
            src_ref=send3.at[k, d - 1], dst_ref=recv3.at[k, d - 1],
            send_sem=s3_send.at[k, d - 1], recv_sem=s3_recv.at[k, d - 1],
            device_id={"col": to}, device_id_type=MESH)

    def multiply(k):
        weight_copy(k).wait()
        pa = jnp.dot(xq[:, :cut], wv[k, :cut], preferred_element_type=F32)
        pb = jnp.dot(xq[:, cut:], wv[k, cut:], preferred_element_type=F32)
        p = pa + pb
        p1, p2 = p[quarter:half], p[half:half + quarter]
        swap = near_first(k)
        send1[k, :quarter] = p[:quarter].astype(BF16)
        send1[k, quarter:] = jnp.where(swap, p2, p1).astype(BF16)
        copy1(k).start()
        own[k, :quarter] = jnp.where(swap, p1, p2)
        own[k, quarter:] = p[half + quarter:]

    def add1(k):
        copy1(k).wait_recv()
        send2[k] = (own[k, :quarter] + recv1[k, :quarter].astype(F32)).astype(BF16)
        copy2(k).start()
        own[k, quarter:] = own[k, quarter:] + recv1[k, quarter:].astype(F32)

    def add2(k):
        copy2(k).wait_recv()
        s = own[k, quarter:] + recv2[k].astype(F32)
        for d in range(1, n_far):
            send3[k, d - 1] = s[d * block:(d + 1) * block].astype(BF16)
            copy3(k, d).start()
        own[k, :block] = s[:block]

    def add3(k):
        s = own[k, :block]
        for d in range(1, n_far):
            copy3(k, d).wait_recv()
            s = s + recv3[k, d - 1].astype(F32)
        m = jnp.max(jnp.abs(s), axis=0, keepdims=True)
        for j in range(CHUNK // LANES):
            mx[...] = jnp.maximum(mx[...], m[:, j * LANES:(j + 1) * LANES])
        cols = pl.ds(pl.multiple_of(k * CHUNK, CHUNK), CHUNK)
        out_ref[:, cols] = jnp.clip(s / previous, -1.0, 1.0).astype(BF16)

    def step(k, carry):
        def at(lag, do):
            pl.when(jnp.logical_and(k >= lag, k < chunks + lag))(lambda: do(k - lag))
        at(0, multiply)
        at(LAG, add1)
        at(2 * LAG, add2)
        at(3 * LAG, add3)
        return carry

    lax.fori_loop(0, chunks + 3 * LAG, step, 0)

    mrec[me] = mx[...]

    def max_copy(i, p, slot):
        return pltpu.make_async_remote_copy(
            src_ref=mx, dst_ref=mrec.at[slot], send_sem=m_send.at[i],
            recv_sem=m_recv.at[slot], device_id=place(p), device_id_type=MESH)

    each_peer(lambda i, p: max_copy(i, p, me).start())

    def sent(k, carry):
        copy1(k).wait_send()
        copy2(k).wait_send()
        for d in range(1, n_far):
            copy3(k, d).wait_send()
        return carry

    lax.fori_loop(0, chunks, sent, 0)
    each_peer(lambda i, p: peak_copy(i, p, me).wait_send())
    for copy in acts_copies:
        copy.wait_send()
    each_peer(lambda i, p: max_copy(i, p, p).wait_recv())
    hist_out[0] = jnp.max(mrec[...])
    for i in range(1, hist_ref.shape[0]):
        hist_out[i] = hist_ref[i - 1]
    each_peer(lambda i, p: max_copy(i, p, me).wait_send())


def write_out(a_ref, b_ref, c_ref, a_out, b_out, c_out, sems):
    pairs = ((a_ref, a_out), (b_ref, b_out), (c_ref, c_out))
    copies = [pltpu.make_async_copy(a, b, sems.at[i]) for i, (a, b) in enumerate(pairs)]
    for copy in copies:
        copy.start()
    for copy in copies:
        copy.wait()


def on_device(n_row, n_col, hidden_acts, down_weight, amax_history):
    rows, depth = hidden_acts.shape
    width = down_weight.shape[1]
    groups = rows // LANES
    tokens = rows * n_row
    half, block, chunks, n_far = tokens // 2, tokens // n_col, width // CHUNK, n_col // 4
    peers = n_row * n_col
    dma = pltpu.SemaphoreType.DMA
    vmem = pl.BlockSpec(memory_space=pltpu.VMEM)
    smem = pl.BlockSpec(memory_space=pltpu.SMEM)
    anywhere = pl.BlockSpec(memory_space=pl.ANY)
    out_shape = (
        jax.ShapeDtypeStruct((block, width), BF16),
        jax.ShapeDtypeStruct((groups, LANES), F32),
        jax.ShapeDtypeStruct(amax_history.shape, F32),
    )
    results = pl.pallas_call(
        functools.partial(kernel, n_row, n_col),
        out_shape=out_shape,
        in_specs=[anywhere, anywhere, smem],
        out_specs=(vmem, vmem, smem),
        scratch_shapes=[
            pltpu.VMEM((tokens, depth), BF16),
            pltpu.VMEM((tokens, depth), BF16),
            pltpu.VMEM((tokens, LANES), BF16),
            pltpu.VMEM((chunks, depth, CHUNK), BF16),
            pltpu.VMEM((groups, LANES), F32),
            pltpu.VMEM((peers, groups, LANES), F32),
            pltpu.VMEM((chunks, half, CHUNK), BF16),
            pltpu.VMEM((chunks, half, CHUNK), BF16),
            pltpu.VMEM((chunks, half, CHUNK), F32),
            pltpu.VMEM((chunks, half // 2, CHUNK), BF16),
            pltpu.VMEM((chunks, half // 2, CHUNK), BF16),
            pltpu.VMEM((chunks, n_far - 1, block, CHUNK), BF16),
            pltpu.VMEM((chunks, n_far - 1, block, CHUNK), BF16),
            pltpu.VMEM((1, LANES), F32),
            pltpu.VMEM((peers, 1, LANES), F32),
            dma, dma((2, n_row - 1)), dma((chunks,)), dma((peers,)), dma((peers,)),
            dma((2, chunks)), dma((2, chunks)), dma((chunks, n_far - 1)), dma((chunks, n_far - 1)),
            dma((peers,)), dma((peers,)),
        ],
        compiler_params=pltpu.CompilerParams(
            collective_id=0, has_side_effects=True, vmem_limit_bytes=56 << 20),
        cost_estimate=pl.CostEstimate(
            flops=2 * tokens * depth * width, bytes_accessed=2 * depth * width, transcendentals=0),
    )(hidden_acts, down_weight, amax_history)
    scaled_out, scale, history = pl.pallas_call(
        write_out, out_shape=out_shape, in_specs=[anywhere] * 3, out_specs=(anywhere,) * 3,
        scratch_shapes=[dma((3,))],
        compiler_params=pltpu.CompilerParams(vmem_limit_bytes=60 << 20),
    )(*results)
    return scaled_out, scale.reshape(rows), history


def solution(mesh):
    in_specs = (P(("grp", "row"), "col"), P("col", "row"), P("grp"))
    out_specs = (P(("grp", "col"), "row"), P(("grp", "row")), P("grp"))
    return jax.shard_map(
        functools.partial(on_device, mesh.shape["row"], mesh.shape["col"]),
        mesh=mesh, in_specs=in_specs, out_specs=out_specs, check_vma=False)
```

```python
import functools

import jax
import jax.numpy as jnp
from jax import lax
from jax.experimental import pallas as pl
from jax.experimental.pallas import tpu as pltpu
from jax.sharding import PartitionSpec as P

clip_ratio = 0.5
format_limit = 448.0
LANES = 128
CHUNK = 256
LAGS = (5, 8, 11)
EARLY = 4
MESH = pl.DeviceIdType.MESH
F32 = jnp.float32
BF16 = jnp.bfloat16


def kernel(
    n_row, n_col,
    h_ref, w_ref, hist_ref,
    out_ref, scale_ref, hist_out,
    hq, xq, lim, wv, pk, prec, send1, recv1, own, send2, recv2, send3, recv3, mx, mrec,
    h_sem, hr_sem, w_sem, pk_send, pk_recv, s1_sem, s2_sem, s3_send, s3_recv, m_send, m_recv,
):
    rows, depth = h_ref.shape
    groups = rows // LANES
    chunks = wv.shape[0]
    n_far = n_col // 4
    half = rows * n_row // 2
    quarter = half // 2
    block = rows * n_row // n_col
    peers = n_row * n_col
    r, c = lax.axis_index("row"), lax.axis_index("col")
    far, near, y = c // 4, lax.rem(c // 2, 2), lax.rem(c, 2)
    me = r * n_col + c
    my_rows = pl.ds(pl.multiple_of(r * rows, LANES), rows)

    def place(p):
        return {"row": p // n_col, "col": lax.rem(p, n_col)}

    def each_peer(do):
        def body(o, carry):
            do(o - 1, lax.rem(me + o, peers))
            return carry
        lax.fori_loop(1, peers, body, 0)

    barrier = pltpu.get_barrier_semaphore()
    each_peer(lambda i, p: pl.semaphore_signal(
        barrier, inc=1, device_id=place(p), device_id_type=MESH))

    own_copy = pltpu.make_async_copy(h_ref, hq.at[my_rows], h_sem)
    own_copy.start()

    def weight_copy(k):
        cols = pl.ds(pl.multiple_of(k * CHUNK, CHUNK), CHUNK)
        return pltpu.make_async_copy(w_ref.at[:, cols], wv.at[k], w_sem.at[k])

    acts_copies = []
    for o in range(1, n_row):
        to = lax.rem(r + o, n_row)
        acts_copies.append(pltpu.make_async_remote_copy(
            src_ref=hq.at[my_rows], dst_ref=hq.at[my_rows], send_sem=hr_sem.at[0, o - 1],
            recv_sem=hr_sem.at[1, o - 1], device_id={"row": to}, device_id_type=MESH))

    own_copy.wait()
    for k in range(EARLY):
        weight_copy(k).start()
    pl.semaphore_wait(barrier, peers - 1)
    for copy in acts_copies:
        copy.start()

    whole = depth // LANES
    for g in range(groups):
        at = pl.ds(pl.multiple_of(r * rows + g * LANES, LANES), LANES)
        m = jnp.abs(hq[at, 0:LANES])
        for j in range(1, whole):
            m = jnp.maximum(m, jnp.abs(hq[at, j * LANES:(j + 1) * LANES]))
        m = m.astype(F32)
        if depth % LANES:
            tail = jnp.abs(hq[at, whole * LANES:].astype(F32))
            m = jnp.maximum(m, jnp.max(tail, axis=1, keepdims=True))
        peak = jnp.max(jnp.transpose(m), axis=0, keepdims=True)
        pk[g:g + 1, :] = peak
        prec[me, g:g + 1, :] = peak

    def peak_copy(i, p, slot):
        return pltpu.make_async_remote_copy(
            src_ref=pk, dst_ref=prec.at[slot], send_sem=pk_send.at[i],
            recv_sem=pk_recv.at[slot], device_id=place(p), device_id_type=MESH)

    each_peer(lambda i, p: peak_copy(i, p, me).start())
    for k in range(EARLY, chunks):
        weight_copy(k).start()

    each_peer(lambda i, p: peak_copy(i, p, p).wait_recv())
    for q in range(n_row):
        top = jnp.max(prec[q * n_col:(q + 1) * n_col], axis=0)
        for g in range(groups):
            edge = clip_ratio * (top[g:g + 1] + 1e-06)
            wide = jnp.transpose(jnp.broadcast_to(edge, (LANES, LANES)))
            at = q * rows + g * LANES
            lim[at:at + LANES, :] = wide.astype(BF16)
    mine = jnp.max(prec[pl.ds(r * n_col, n_col)], axis=0)
    scale_ref[...] = clip_ratio * (mine + 1e-06) / format_limit

    for copy in acts_copies:
        copy.wait_recv()

    def clip_block(b, carry):
        part, d = b // n_far, lax.rem(b, n_far)
        to_y = lax.rem(y + 1 - part // 2, 2)
        to_near = lax.rem(near + 1 - lax.rem(part, 2), 2)
        col_at = 4 * lax.rem(far + d, n_far) + 2 * to_near + to_y
        src = pl.ds(pl.multiple_of(col_at * block, block), block)
        dst = pl.ds(pl.multiple_of(b * block, block), block)
        edge = lim[src, :]
        for j in range(pl.cdiv(depth, LANES)):
            lo, hi = j * LANES, min((j + 1) * LANES, depth)
            e = edge[:, :hi - lo]
            xq[dst, lo:hi] = jnp.minimum(jnp.maximum(hq[src, lo:hi], -e), e)
        return carry

    lax.fori_loop(0, n_col, clip_block, 0)

    previous = hist_ref[0]
    for i in range(1, hist_ref.shape[0]):
        previous = jnp.maximum(previous, hist_ref[i])
    mx[...] = jnp.zeros_like(mx)

    y_peer = 4 * far + 2 * near + 1 - y
    near_peer = 4 * far + 2 * (1 - near) + y

    def near_first(k):
        return jnp.logical_and(k < 6, lax.rem(k, 2) == 1)

    def copy1(k):
        return pltpu.make_async_remote_copy(
            src_ref=send1.at[k], dst_ref=recv1.at[k], send_sem=s1_sem.at[0, k],
            recv_sem=s1_sem.at[1, k], device_id_type=MESH,
            device_id={"col": jnp.where(near_first(k), near_peer, y_peer)})

    def copy2(k):
        return pltpu.make_async_remote_copy(
            src_ref=send2.at[k], dst_ref=recv2.at[k], send_sem=s2_sem.at[0, k],
            recv_sem=s2_sem.at[1, k], device_id_type=MESH,
            device_id={"col": jnp.where(near_first(k), y_peer, near_peer)})

    def copy3(k, d):
        to = 4 * lax.rem(far + d, n_far) + 2 * near + y
        return pltpu.make_async_remote_copy(
            src_ref=send3.at[k, d - 1], dst_ref=recv3.at[k, d - 1],
            send_sem=s3_send.at[k, d - 1], recv_sem=s3_recv.at[k, d - 1],
            device_id={"col": to}, device_id_type=MESH)

    def multiply(k):
        weight_copy(k).wait()
        p = jnp.dot(xq[...], wv[k], preferred_element_type=F32)
        p1, p2 = p[quarter:half], p[half:half + quarter]
        swap = near_first(k)
        send1[k, :quarter] = p[:quarter].astype(BF16)
        send1[k, quarter:] = jnp.where(swap, p2, p1).astype(BF16)
        copy1(k).start()
        own[k, :quarter] = jnp.where(swap, p1, p2)
        own[k, quarter:] = p[half + quarter:]

    def add1(k):
        copy1(k).wait_recv()
        send2[k] = (own[k, :quarter] + recv1[k, :quarter].astype(F32)).astype(BF16)
        copy2(k).start()
        own[k, quarter:] = own[k, quarter:] + recv1[k, quarter:].astype(F32)

    def add2(k):
        copy2(k).wait_recv()
        s = own[k, quarter:] + recv2[k].astype(F32)
        for d in range(1, n_far):
            send3[k, d - 1] = s[d * block:(d + 1) * block].astype(BF16)
            copy3(k, d).start()
        own[k, :block] = s[:block]

    def add3(k):
        s = own[k, :block]
        for d in range(1, n_far):
            copy3(k, d).wait_recv()
            s = s + recv3[k, d - 1].astype(F32)
        m = jnp.max(jnp.abs(s), axis=0, keepdims=True)
        for j in range(CHUNK // LANES):
            mx[...] = jnp.maximum(mx[...], m[:, j * LANES:(j + 1) * LANES])
        cols = pl.ds(pl.multiple_of(k * CHUNK, CHUNK), CHUNK)
        out_ref[:, cols] = jnp.clip(s / previous, -1.0, 1.0).astype(BF16)

    def step(k, carry):
        def at(lag, do):
            pl.when(jnp.logical_and(k >= lag, k < chunks + lag))(lambda: do(k - lag))
        at(0, multiply)
        at(LAGS[0], add1)
        at(LAGS[1], add2)
        at(LAGS[2], add3)
        return carry

    lax.fori_loop(0, chunks + LAGS[2], step, 0)

    mrec[me] = mx[...]

    def max_copy(i, p, slot):
        return pltpu.make_async_remote_copy(
            src_ref=mx, dst_ref=mrec.at[slot], send_sem=m_send.at[i],
            recv_sem=m_recv.at[slot], device_id=place(p), device_id_type=MESH)

    each_peer(lambda i, p: max_copy(i, p, me).start())

    def sent(k, carry):
        copy1(k).wait_send()
        copy2(k).wait_send()
        for d in range(1, n_far):
            copy3(k, d).wait_send()
        return carry

    lax.fori_loop(0, chunks, sent, 0)
    each_peer(lambda i, p: peak_copy(i, p, me).wait_send())
    for copy in acts_copies:
        copy.wait_send()
    each_peer(lambda i, p: max_copy(i, p, p).wait_recv())
    hist_out[0] = jnp.max(mrec[...])
    for i in range(1, hist_ref.shape[0]):
        hist_out[i] = hist_ref[i - 1]
    each_peer(lambda i, p: max_copy(i, p, me).wait_send())


def write_out(a_ref, b_ref, c_ref, a_out, b_out, c_out):
    a_out[...] = a_ref[...]
    b_out[...] = b_ref[...]
    for i in range(c_ref.shape[0]):
        c_out[i] = c_ref[i]


def on_device(n_row, n_col, hidden_acts, down_weight, amax_history):
    rows, depth = hidden_acts.shape
    width = down_weight.shape[1]
    groups = rows // LANES
    tokens = rows * n_row
    half, block, chunks, n_far = tokens // 2, tokens // n_col, width // CHUNK, n_col // 4
    peers = n_row * n_col
    dma = pltpu.SemaphoreType.DMA
    vmem = pl.BlockSpec(memory_space=pltpu.VMEM)
    smem = pl.BlockSpec(memory_space=pltpu.SMEM)
    anywhere = pl.BlockSpec(memory_space=pl.ANY)
    out_shape = (
        jax.ShapeDtypeStruct((block, width), BF16),
        jax.ShapeDtypeStruct((groups, LANES), F32),
        jax.ShapeDtypeStruct(amax_history.shape, F32),
    )
    results = pl.pallas_call(
        functools.partial(kernel, n_row, n_col),
        out_shape=out_shape,
        in_specs=[anywhere, anywhere, smem],
        out_specs=(vmem, vmem, smem),
        scratch_shapes=[
            pltpu.VMEM((tokens, depth), BF16),
            pltpu.VMEM((tokens, depth), BF16),
            pltpu.VMEM((tokens, LANES), BF16),
            pltpu.VMEM((chunks, depth, CHUNK), BF16),
            pltpu.VMEM((groups, LANES), F32),
            pltpu.VMEM((peers, groups, LANES), F32),
            pltpu.VMEM((chunks, half, CHUNK), BF16),
            pltpu.VMEM((chunks, half, CHUNK), BF16),
            pltpu.VMEM((chunks, half, CHUNK), F32),
            pltpu.VMEM((chunks, half // 2, CHUNK), BF16),
            pltpu.VMEM((chunks, half // 2, CHUNK), BF16),
            pltpu.VMEM((chunks, n_far - 1, block, CHUNK), BF16),
            pltpu.VMEM((chunks, n_far - 1, block, CHUNK), BF16),
            pltpu.VMEM((1, LANES), F32),
            pltpu.VMEM((peers, 1, LANES), F32),
            dma, dma((2, n_row - 1)), dma((chunks,)), dma((peers,)), dma((peers,)),
            dma((2, chunks)), dma((2, chunks)), dma((chunks, n_far - 1)), dma((chunks, n_far - 1)),
            dma((peers,)), dma((peers,)),
        ],
        compiler_params=pltpu.CompilerParams(
            collective_id=0, has_side_effects=True, vmem_limit_bytes=56 << 20),
        cost_estimate=pl.CostEstimate(
            flops=2 * tokens * depth * width, bytes_accessed=2 * depth * width, transcendentals=0),
    )(hidden_acts, down_weight, amax_history)
    scaled_out, scale, history = pl.pallas_call(
        write_out, out_shape=out_shape, in_specs=[vmem, vmem, smem], out_specs=(vmem, vmem, smem),
        compiler_params=pltpu.CompilerParams(vmem_limit_bytes=60 << 20),
    )(*results)
    return scaled_out, scale.reshape(rows), history


def solution(mesh):
    in_specs = (P(("grp", "row"), "col"), P("col", "row"), P("grp"))
    out_specs = (P(("grp", "col"), "row"), P(("grp", "row")), P("grp"))
    return jax.shard_map(
        functools.partial(on_device, mesh.shape["row"], mesh.shape["col"]),
        mesh=mesh, in_specs=in_specs, out_specs=out_specs, check_vma=False)
```

```python
import functools

import jax
import jax.numpy as jnp
from jax import lax
from jax.experimental import pallas as pl
from jax.experimental.pallas import tpu as pltpu
from jax.sharding import PartitionSpec as P

clip_ratio = 0.5
format_limit = 448.0
LANES = 128
CHUNK = 256
LAGS = (5, 8, 11)
WIDE = 4
MESH = pl.DeviceIdType.MESH
F32 = jnp.float32
BF16 = jnp.bfloat16


def kernel(
    n_row, n_col,
    h_ref, w_ref, hist_ref,
    out_ref, scale_ref, hist_out,
    hq, xq, lim, wv, pk, prec, send1, recv1, own, send2, recv2, send3, recv3, mx, mrec,
    h_sem, hr_sem, w_sem, pk_send, pk_recv, s1_sem, s2_sem, s3_send, s3_recv, m_send, m_recv,
):
    rows, depth = h_ref.shape
    groups = rows // LANES
    chunks = wv.shape[0] * WIDE
    n_far = n_col // 4
    half = rows * n_row // 2
    quarter = half // 2
    block = rows * n_row // n_col
    peers = n_row * n_col
    r, c = lax.axis_index("row"), lax.axis_index("col")
    far, near, y = c // 4, lax.rem(c // 2, 2), lax.rem(c, 2)
    me = r * n_col + c
    my_rows = pl.ds(pl.multiple_of(r * rows, LANES), rows)

    def place(p):
        return {"row": p // n_col, "col": lax.rem(p, n_col)}

    def each_peer(do):
        def body(o, carry):
            do(o - 1, lax.rem(me + o, peers))
            return carry
        lax.fori_loop(1, peers, body, 0)

    barrier = pltpu.get_barrier_semaphore()
    each_peer(lambda i, p: pl.semaphore_signal(
        barrier, inc=1, device_id=place(p), device_id_type=MESH))

    own_copy = pltpu.make_async_copy(h_ref, hq.at[my_rows], h_sem)
    own_copy.start()

    def weight_copy(k):
        cols = pl.ds(pl.multiple_of(k * WIDE * CHUNK, CHUNK), WIDE * CHUNK)
        return pltpu.make_async_copy(w_ref.at[:, cols], wv.at[k], w_sem.at[k])

    acts_copies = []
    for o in range(1, n_row):
        to = lax.rem(r + o, n_row)
        acts_copies.append(pltpu.make_async_remote_copy(
            src_ref=hq.at[my_rows], dst_ref=hq.at[my_rows], send_sem=hr_sem.at[0, o - 1],
            recv_sem=hr_sem.at[1, o - 1], device_id={"row": to}, device_id_type=MESH))

    own_copy.wait()
    weight_copy(0).start()
    pl.semaphore_wait(barrier, peers - 1)
    for copy in acts_copies:
        copy.start()

    whole = depth // LANES
    for g in range(groups):
        at = pl.ds(pl.multiple_of(r * rows + g * LANES, LANES), LANES)
        m = jnp.abs(hq[at, 0:LANES])
        for j in range(1, whole):
            m = jnp.maximum(m, jnp.abs(hq[at, j * LANES:(j + 1) * LANES]))
        m = m.astype(F32)
        if depth % LANES:
            tail = jnp.abs(hq[at, whole * LANES:].astype(F32))
            m = jnp.maximum(m, jnp.max(tail, axis=1, keepdims=True))
        peak = jnp.max(jnp.transpose(m), axis=0, keepdims=True)
        pk[g:g + 1, :] = peak
        prec[me, g:g + 1, :] = peak

    def peak_copy(i, p, slot):
        return pltpu.make_async_remote_copy(
            src_ref=pk, dst_ref=prec.at[slot], send_sem=pk_send.at[i],
            recv_sem=pk_recv.at[slot], device_id=place(p), device_id_type=MESH)

    each_peer(lambda i, p: peak_copy(i, p, me).start())
    for k in range(1, chunks // WIDE):
        weight_copy(k).start()

    each_peer(lambda i, p: peak_copy(i, p, p).wait_recv())
    for q in range(n_row):
        top = jnp.max(prec[q * n_col:(q + 1) * n_col], axis=0)
        for g in range(groups):
            edge = clip_ratio * (top[g:g + 1] + 1e-06)
            wide = jnp.transpose(jnp.broadcast_to(edge, (LANES, LANES)))
            at = q * rows + g * LANES
            lim[at:at + LANES, :] = wide.astype(BF16)
    mine = jnp.max(prec[pl.ds(r * n_col, n_col)], axis=0)
    scale_ref[...] = clip_ratio * (mine + 1e-06) / format_limit

    for copy in acts_copies:
        copy.wait_recv()

    def clip_block(b, carry):
        part, d = b // n_far, lax.rem(b, n_far)
        to_y = lax.rem(y + 1 - part // 2, 2)
        to_near = lax.rem(near + 1 - lax.rem(part, 2), 2)
        col_at = 4 * lax.rem(far + d, n_far) + 2 * to_near + to_y
        src = pl.ds(pl.multiple_of(col_at * block, block), block)
        dst = pl.ds(pl.multiple_of(b * block, block), block)
        edge = lim[src, :]
        for j in range(pl.cdiv(depth, LANES)):
            lo, hi = j * LANES, min((j + 1) * LANES, depth)
            e = edge[:, :hi - lo]
            xq[dst, lo:hi] = jnp.minimum(jnp.maximum(hq[src, lo:hi], -e), e)
        return carry

    lax.fori_loop(0, n_col, clip_block, 0)

    previous = hist_ref[0]
    for i in range(1, hist_ref.shape[0]):
        previous = jnp.maximum(previous, hist_ref[i])
    mx[...] = jnp.zeros_like(mx)

    y_peer = 4 * far + 2 * near + 1 - y
    near_peer = 4 * far + 2 * (1 - near) + y

    def near_first(k):
        return lax.rem(k, 4) == 1

    def copy1(k):
        return pltpu.make_async_remote_copy(
            src_ref=send1.at[k], dst_ref=recv1.at[k], send_sem=s1_sem.at[0, k],
            recv_sem=s1_sem.at[1, k], device_id_type=MESH,
            device_id={"col": jnp.where(near_first(k), near_peer, y_peer)})

    def copy2(k):
        return pltpu.make_async_remote_copy(
            src_ref=send2.at[k], dst_ref=recv2.at[k], send_sem=s2_sem.at[0, k],
            recv_sem=s2_sem.at[1, k], device_id_type=MESH,
            device_id={"col": jnp.where(near_first(k), y_peer, near_peer)})

    def copy3(k, d):
        to = 4 * lax.rem(far + d, n_far) + 2 * near + y
        return pltpu.make_async_remote_copy(
            src_ref=send3.at[k, d - 1], dst_ref=recv3.at[k, d - 1],
            send_sem=s3_send.at[k, d - 1], recv_sem=s3_recv.at[k, d - 1],
            device_id={"col": to}, device_id_type=MESH)

    def multiply(k):
        pl.when(lax.rem(k, WIDE) == 0)(lambda: weight_copy(k // WIDE).wait())
        cols = pl.ds(pl.multiple_of(lax.rem(k, WIDE) * CHUNK, CHUNK), CHUNK)
        p = jnp.dot(xq[...], wv[k // WIDE, :, cols], preferred_element_type=F32)
        p1, p2 = p[quarter:half], p[half:half + quarter]
        swap = near_first(k)
        send1[k, :quarter] = p[:quarter].astype(BF16)
        send1[k, quarter:] = jnp.where(swap, p2, p1).astype(BF16)
        copy1(k).start()
        own[k, :quarter] = jnp.where(swap, p1, p2)
        own[k, quarter:] = p[half + quarter:]

    def add1(k):
        copy1(k).wait_recv()
        send2[k] = (own[k, :quarter] + recv1[k, :quarter].astype(F32)).astype(BF16)
        copy2(k).start()
        own[k, quarter:] = own[k, quarter:] + recv1[k, quarter:].astype(F32)

    def add2(k):
        copy2(k).wait_recv()
        s = own[k, quarter:] + recv2[k].astype(F32)
        for d in range(1, n_far):
            send3[k, d - 1] = s[d * block:(d + 1) * block].astype(BF16)
            copy3(k, d).start()
        own[k, :block] = s[:block]

    def add3(k):
        s = own[k, :block]
        for d in range(1, n_far):
            copy3(k, d).wait_recv()
            s = s + recv3[k, d - 1].astype(F32)
        m = jnp.max(jnp.abs(s), axis=0, keepdims=True)
        for j in range(CHUNK // LANES):
            mx[...] = jnp.maximum(mx[...], m[:, j * LANES:(j + 1) * LANES])
        cols = pl.ds(pl.multiple_of(k * CHUNK, CHUNK), CHUNK)
        out_ref[:, cols] = jnp.clip(s / previous, -1.0, 1.0).astype(BF16)

    def step(k, carry):
        def at(lag, do):
            pl.when(jnp.logical_and(k >= lag, k < chunks + lag))(lambda: do(k - lag))
        at(0, multiply)
        at(LAGS[0], add1)
        at(LAGS[1], add2)
        at(LAGS[2], add3)
        return carry

    lax.fori_loop(0, chunks + LAGS[2], step, 0)

    mrec[me] = mx[...]

    def max_copy(i, p, slot):
        return pltpu.make_async_remote_copy(
            src_ref=mx, dst_ref=mrec.at[slot], send_sem=m_send.at[i],
            recv_sem=m_recv.at[slot], device_id=place(p), device_id_type=MESH)

    each_peer(lambda i, p: max_copy(i, p, me).start())

    def sent(k, carry):
        copy1(k).wait_send()
        copy2(k).wait_send()
        for d in range(1, n_far):
            copy3(k, d).wait_send()
        return carry

    lax.fori_loop(0, chunks, sent, 0)
    each_peer(lambda i, p: peak_copy(i, p, me).wait_send())
    for copy in acts_copies:
        copy.wait_send()
    each_peer(lambda i, p: max_copy(i, p, p).wait_recv())
    hist_out[0] = jnp.max(mrec[...])
    for i in range(1, hist_ref.shape[0]):
        hist_out[i] = hist_ref[i - 1]
    each_peer(lambda i, p: max_copy(i, p, me).wait_send())


def write_out(a_ref, b_ref, c_ref, a_out, b_out, c_out):
    a_out[...] = a_ref[...]
    b_out[...] = b_ref[...]
    for i in range(c_ref.shape[0]):
        c_out[i] = c_ref[i]


def on_device(n_row, n_col, hidden_acts, down_weight, amax_history):
    rows, depth = hidden_acts.shape
    width = down_weight.shape[1]
    groups = rows // LANES
    tokens = rows * n_row
    half, block, chunks, n_far = tokens // 2, tokens // n_col, width // CHUNK, n_col // 4
    peers = n_row * n_col
    dma = pltpu.SemaphoreType.DMA
    vmem = pl.BlockSpec(memory_space=pltpu.VMEM)
    smem = pl.BlockSpec(memory_space=pltpu.SMEM)
    anywhere = pl.BlockSpec(memory_space=pl.ANY)
    out_shape = (
        jax.ShapeDtypeStruct((block, width), BF16),
        jax.ShapeDtypeStruct((groups, LANES), F32),
        jax.ShapeDtypeStruct(amax_history.shape, F32),
    )
    results = pl.pallas_call(
        functools.partial(kernel, n_row, n_col),
        out_shape=out_shape,
        in_specs=[anywhere, anywhere, smem],
        out_specs=(vmem, vmem, smem),
        scratch_shapes=[
            pltpu.VMEM((tokens, depth), BF16),
            pltpu.VMEM((tokens, depth), BF16),
            pltpu.VMEM((tokens, LANES), BF16),
            pltpu.VMEM((chunks // WIDE, depth, WIDE * CHUNK), BF16),
            pltpu.VMEM((groups, LANES), F32),
            pltpu.VMEM((peers, groups, LANES), F32),
            pltpu.VMEM((chunks, half, CHUNK), BF16),
            pltpu.VMEM((chunks, half, CHUNK), BF16),
            pltpu.VMEM((chunks, half, CHUNK), F32),
            pltpu.VMEM((chunks, half // 2, CHUNK), BF16),
            pltpu.VMEM((chunks, half // 2, CHUNK), BF16),
            pltpu.VMEM((chunks, n_far - 1, block, CHUNK), BF16),
            pltpu.VMEM((chunks, n_far - 1, block, CHUNK), BF16),
            pltpu.VMEM((1, LANES), F32),
            pltpu.VMEM((peers, 1, LANES), F32),
            dma, dma((2, n_row - 1)), dma((chunks // WIDE,)), dma((peers,)), dma((peers,)),
            dma((2, chunks)), dma((2, chunks)), dma((chunks, n_far - 1)), dma((chunks, n_far - 1)),
            dma((peers,)), dma((peers,)),
        ],
        compiler_params=pltpu.CompilerParams(
            collective_id=0, has_side_effects=True, vmem_limit_bytes=56 << 20),
        cost_estimate=pl.CostEstimate(
            flops=2 * tokens * depth * width, bytes_accessed=2 * depth * width, transcendentals=0),
    )(hidden_acts, down_weight, amax_history)
    scaled_out, scale, history = pl.pallas_call(
        write_out, out_shape=out_shape, in_specs=[vmem, vmem, smem], out_specs=(vmem, vmem, smem),
        compiler_params=pltpu.CompilerParams(vmem_limit_bytes=60 << 20),
    )(*results)
    return scaled_out, scale.reshape(rows), history


def solution(mesh):
    in_specs = (P(("grp", "row"), "col"), P("col", "row"), P("grp"))
    out_specs = (P(("grp", "col"), "row"), P(("grp", "row")), P("grp"))
    return jax.shard_map(
        functools.partial(on_device, mesh.shape["row"], mesh.shape["col"]),
        mesh=mesh, in_specs=in_specs, out_specs=out_specs, check_vma=False)
```
